128 devices in a mesh: glob: 8 (over x, y_lo), reg: 16 (over z, y_hi, core).
Axes of the slice: x: 4, y: 4 (y_hi: 2, y_lo: 2; y = y_hi * 2 + y_lo), z: 4, core: 2. Of those that a mesh axis runs over, the one named last changes fastest.
Arguments:
- global_state: bfloat16 [128, 1024, 512], P('glob', 'reg'), may hold values from -6 to 6
- norm_gain: float32 [512], replicated, may hold values from 0.1 to 1.9
- qkv_weight: bfloat16 [512, 1536], replicated, may hold values from -0.25 to 0.25
- out_weight: bfloat16 [512, 512], replicated, may hold values from -0.25 to 0.25
- position_bias: float32 [8, 128, 128], replicated, may hold values from -4 to 262
- regional_state: bfloat16 [99, 128, 2048], P(None, 'glob', 'reg'), may hold values from -6 to 6
- conv_state: bfloat16 [9, 256, 99], replicated, may hold values from -0.1875 to 0.1875
- cond_weight: bfloat16 [256, 512], replicated, may hold values from -0.25 to 0.25
- conv_mid: bfloat16 [9, 256, 256], replicated, may hold values from -0.125 to 0.125
- conv_out: bfloat16 [9, 99, 256], replicated, may hold values from -0.125 to 0.125
- blocks: bfloat16 [64, 2048], replicated, may hold values from 0 to 0.25
- sources: int32 [8, 16, 64], P('glob', 'reg'), may hold values from 0 to 131071, as said below
- block_ids: int32 [8, 16, 64], P('glob', 'reg'), may hold values from 0 to 63, each once within a row
- shift_offset: int32 [1], replicated, may hold values from 1 to 7
Outputs:
- global_next: bfloat16 [128, 1024, 512], P('glob', 'reg')
- regional_next: float32 [99, 128, 2048], P(None, 'glob', 'reg')
The draws below stay inside these ranges and needn't reach their ends.
Inputs may be any that keep to these rules, and one draw needn't show every extreme that they name: sources[i, j, :] belongs to the tile in tile row i, tile column j and gives global tokens as row * 1024 + column; it names only tokens of latitude band i (global rows i * 16 to i * 16 + 15); all tiles name only tokens of two neighbouring longitude sectors, global columns s * 64 to s * 64 + 2 * 64 - 1 for one s, and every tile names some token of each of these two sectors. `block_ids`: each tile names every block once.
All inputs are finite; a program needn't handle non-finite values.
Results may differ from the reference program's by a relative error of at most 0.006.
Values may be sent and summed in bfloat16 or wider, within the bound.
A program may use at most 128 MiB of HBM per device.

```python
import jax
import jax.numpy as jnp
from jax import lax

CG = 512
HG = 8
CS = 99
C = 256
WH = 8
WL = 16
WT = 128
GB = 16
GL = 64
TH = 16
TW = 128
K = 64
CELLS = 2048
GLAT = 128
GLON = 1024
RY = 128
RX = 2048
N_GLOB = 8
N_REG = 16


def draw_position_bias(key, part):
    key = jax.random.fold_in(key, 11)
    base_key = jax.random.fold_in(key, 0)
    bias_table = jnp.clip(jax.random.normal(base_key, (HG, WT, WT), jnp.float32), -4.0, 4.0)
    return bias_table.astype(jnp.float32)


def draw_sources(key, part):
    key = jax.random.fold_in(key, 5)
    sector_key, row_key, col_key = jax.random.split(key, 3)
    bands = GLAT // GB
    sectors = GLON // GL
    first_sector = jax.random.randint(sector_key, (), 0, sectors - 1)
    band_rows = jax.random.randint(row_key, (bands, sectors, K), 0, GB)
    offsets = jax.random.randint(col_key, (bands, sectors, K), 0, 2 * GL)
    slot_ids = jnp.arange(K)[None, None, :]
    offsets = jnp.where(slot_ids == 0, offsets % GL, jnp.where(slot_ids == 1, GL + offsets % GL, offsets))
    rows_all = jnp.arange(bands)[:, None, None] * GB + band_rows
    return (rows_all * GLON + first_sector * GL + offsets).astype(jnp.int32)


def levels(own_key, extent, cuts, low, largest):
    loudness = 1.0
    for axis_at, shards_of in cuts:
        heights = jax.random.uniform(jax.random.fold_in(jax.random.fold_in(own_key, 6), axis_at), (shards_of,), jnp.float32, low / len(cuts), largest / len(cuts))
        loudness = loudness * jnp.repeat(jnp.exp(heights), extent[axis_at] // shards_of).reshape((-1,) + (1,) * (len(extent) - 1 - axis_at))
    return loudness


def gaussian(rng, shape, deviation, limit, cuts=(), held_as=jnp.bfloat16):
    gain = levels(rng, shape, cuts, -0.22, 0.18) if cuts else 1.0
    array = jax.random.normal(rng, shape, jnp.float32) * deviation * gain
    return jnp.minimum(jnp.maximum(array, -limit), limit).astype(held_as)


def setup_inputs(seed: int = 0) -> dict:
    seeds = jax.random.split(jax.random.key(seed), 15)
    global_state = gaussian(seeds[0], (GLAT, GLON, CG), 1.0, 6.0, ((0, 8), (1, 16)))
    norm_gain = jnp.clip(1.0 + 0.18 * jax.random.normal(seeds[1], (CG,), jnp.float32), 0.1, 1.9)
    qkv_weight = gaussian(seeds[2], (CG, 3 * CG), CG ** -0.5, 0.25)
    out_weight = gaussian(seeds[3], (CG, CG), CG ** -0.5, 0.25)
    position_bias = draw_position_bias(jax.random.fold_in(seeds[14], 71), 0)
    regional_state = gaussian(seeds[5], (CS, RY, RX), 1.0, 6.0, ((1, 8), (2, 16)))
    conv_state = gaussian(seeds[6], (9, C, CS), (9 * CS) ** -0.5, 0.1875)
    cond_weight = gaussian(seeds[7], (C, CG), CG ** -0.5, 0.25)
    conv_mid = gaussian(seeds[8], (9, C, C), (9 * C) ** -0.5, 0.125)
    conv_out = gaussian(seeds[9], (9, CS, C), (9 * C) ** -0.5, 0.125)
    blocks = jnp.clip(jax.random.uniform(seeds[10], (K, CELLS), jnp.float32, 0.0, 0.25), 0.0, 0.25).astype(jnp.bfloat16)
    sources = draw_sources(jax.random.fold_in(seeds[14], 71), 0)
    block_ids = jax.vmap(lambda own: jax.random.permutation(own, K))(jax.random.split(seeds[12], N_GLOB * N_REG)).reshape((N_GLOB, N_REG, K)).astype(jnp.int32)
    shift_offset = jax.random.randint(seeds[13], (1,), 1, WH).astype(jnp.int32)
    return {"global_state": global_state, "norm_gain": norm_gain, "qkv_weight": qkv_weight, "out_weight": out_weight, "position_bias": position_bias, "regional_state": regional_state, "conv_state": conv_state, "cond_weight": cond_weight, "conv_mid": conv_mid, "conv_out": conv_out, "blocks": blocks, "sources": sources, "block_ids": block_ids, "shift_offset": shift_offset}


def layer_norm(tokens_in, norm_gain):
    values = tokens_in.astype(jnp.float32)
    center = values - lax.optimization_barrier(jnp.mean(values, axis=-1, keepdims=True))
    spread = lax.optimization_barrier(jnp.mean(center * center, axis=-1, keepdims=True))
    return (center * lax.rsqrt(spread + 1e-05) * norm_gain).astype(jnp.bfloat16)

def attend(queries, key_pairs, first_row, position_bias):
    span_rows, lanes_all, width = queries.shape
    heads = position_bias.shape[0]
    head_size = width // heads
    stripes = span_rows // WH
    lanes = lanes_all // WL

    def arrange(block_in, depth):
        shaped = block_in.reshape(stripes, WH, lanes, WL, depth).transpose(0, 2, 1, 3, 4)
        return shaped.reshape(stripes, lanes, WH * WL, depth)
    query_win = arrange(queries, width).reshape(stripes, lanes, WH * WL, heads, head_size)
    pair_win = arrange(key_pairs, 2 * width)
    key_win = pair_win[..., :width].reshape(stripes, lanes, WH * WL, heads, head_size)
    value_win = pair_win[..., width:].reshape(stripes, lanes, WH * WL, heads, head_size)
    scores = jnp.einsum('abqhd,abkhd->abhqk', query_win.astype(jnp.float32), key_win.astype(jnp.float32))
    scores = scores * head_size ** (-0.5) + position_bias
    row_ids = first_row + jnp.arange(span_rows, dtype=jnp.int32).reshape(stripes, WH)
    row_valid = (row_ids >= 0) & (row_ids < GLAT)
    key_valid = jnp.repeat(row_valid, WL, axis=1)
    scores = jnp.where(key_valid[:, None, None, None, :], scores, -jnp.inf)
    row_peak = lax.optimization_barrier(jnp.max(scores, axis=-1, keepdims=True))
    scaled_exp = jnp.exp(scores - row_peak)
    weights = (scaled_exp / lax.optimization_barrier(jnp.sum(scaled_exp, axis=-1, keepdims=True))).astype(jnp.bfloat16)
    mixed_win = jnp.einsum('abhqk,abkhd->abqhd', weights.astype(jnp.float32), value_win.astype(jnp.float32))
    mixed_win = mixed_win.astype(jnp.bfloat16).reshape(stripes, lanes, WH, WL, width)
    return mixed_win.transpose(0, 2, 1, 3, 4).reshape(span_rows, lanes_all, width)

def convolve(kernel, grid_in):
    channels, height, breadth = grid_in.shape
    padded = jnp.pad(grid_in, ((0, 0), (1, 1), (1, 1)))
    running = jnp.zeros((kernel.shape[1], height * breadth), jnp.float32)
    for offset in range(9):
        window = padded[:, offset // 3:offset // 3 + height, offset % 3:offset % 3 + breadth]
        running = running + jnp.dot(kernel[offset], window.reshape(channels, height * breadth), preferred_element_type=jnp.float32)
    return running.reshape(kernel.shape[1], height, breadth)

def reference(global_state, norm_gain, qkv_weight, out_weight, position_bias, regional_state, conv_state, cond_weight, conv_mid, conv_out, blocks, sources, block_ids, shift_offset):
    shift_rows = shift_offset[0].astype(jnp.int32)
    normed = layer_norm(global_state, norm_gain)
    projected = jnp.dot(normed.reshape(GLAT * GLON, CG), qkv_weight, preferred_element_type=jnp.float32)
    projected = projected.astype(jnp.bfloat16).reshape(GLAT, GLON, 3 * CG)
    padded = jnp.pad(projected, ((WH, WH), (0, 0), (0, 0)))
    span_block = lax.dynamic_slice_in_dim(padded, (WH - shift_rows).astype(jnp.int32), GLAT + WH, 0)
    stripe_count = GLAT // WH + 1
    stripe_data = span_block.reshape(stripe_count, WH, GLON, 3 * CG)
    stripe_starts = (jnp.arange(stripe_count, dtype=jnp.int32) * WH - shift_rows).astype(jnp.int32)

    def one_stripe(stripe_item):
        stripe, first_row = stripe_item
        return attend(stripe[:, :, :CG], stripe[:, :, CG:], first_row, position_bias)
    mixed_span = lax.map(one_stripe, (stripe_data, stripe_starts)).reshape(GLAT + WH, GLON, CG)
    mixed_rows = lax.dynamic_slice_in_dim(mixed_span, shift_rows, GLAT, 0)
    update = jnp.dot(mixed_rows.reshape(GLAT * GLON, CG), out_weight, preferred_element_type=jnp.float32)
    global_next = (global_state.astype(jnp.float32) + update.reshape(GLAT, GLON, CG)).astype(jnp.bfloat16)
    selected = jnp.take(global_next.reshape(GLAT * GLON, CG), sources.reshape(-1).astype(jnp.int32), axis=0)
    selected = selected.reshape(N_GLOB, N_REG, K, CG)
    chosen_blocks = jnp.take(blocks, block_ids.reshape(-1).astype(jnp.int32), axis=0).reshape(N_GLOB, N_REG, K, CELLS)

    def one_tile(tile_item):
        tile_sel, tile_blocks = tile_item
        return jnp.dot(tile_sel.astype(jnp.float32).T, tile_blocks.astype(jnp.float32)).astype(jnp.bfloat16)
    interp = lax.map(one_tile, (selected.reshape(N_GLOB * N_REG, K, CG), chosen_blocks.reshape(N_GLOB * N_REG, K, CELLS)))
    interp = interp.reshape(N_GLOB, N_REG, CG, TH, TW).transpose(2, 0, 3, 1, 4).reshape(CG, RY * RX)
    cond_term = jnp.dot(cond_weight, interp, preferred_element_type=jnp.float32).reshape(C, RY, RX)
    first_hidden = jax.nn.silu(convolve(conv_state, regional_state) + cond_term).astype(jnp.bfloat16)
    second_hidden = jax.nn.silu(convolve(conv_mid, first_hidden)).astype(jnp.bfloat16)
    regional_next = regional_state.astype(jnp.float32) + convolve(conv_out, second_hidden)
    return (global_next, regional_next)
```

```python
import jax
import jax.numpy as jnp
from jax import lax
from jax.experimental import pallas as pl
from jax.experimental.pallas import tpu as pltpu
from jax.sharding import PartitionSpec as P

MESH = pl.DeviceIdType.MESH
F32 = jnp.float32
BF16 = jnp.bfloat16
NG, NR = 8, 16
PITCH, LEAD = 144, 8
NT = (((1,), (1,)), ((), ()))


def dot(a, b):
    return jnp.dot(a, b, preferred_element_type=F32)


def dot_nt(a, b):
    return lax.dot_general(a, b, NT, preferred_element_type=F32)


def silu(u):
    half = 0.5 * u
    return half + half * jnp.tanh(half)


def rows_at(index, count):
    return pl.ds(pl.multiple_of(index, 16), count)


def body(
    shift_ref, src_ref, bid_ref, gain_ref,
    gs_hbm, rs_hbm, qkvw_hbm, outw_hbm, bias_hbm, cs_hbm, cw_hbm, cm_hbm, co_hbm, blk_hbm,
    gnext_hbm, rnext_hbm,
    own, rsv, qkvw, outw, bias, csv, cw, cmv, cov, blk,
    sb, pb, fb, slab, sg, xs, xn, qkv, mixed, span, onext, yv, sel, zs, zr, z2, zc,
    st32, edge, el, er, rl, rr, xf, x3, hu, hd, p1, w1, w2, w3, amat, xm, x2, ost,
    lsem, psend, precv, fsend, frecv, esend, erecv, hsend, hrecv, gsend, grecv,
    asend, arecv, bsend, brecv, nsend, nrecv, osem,
):
    g = lax.axis_index("glob")
    r = lax.axis_index("reg")
    odd = lax.rem(g, 2)
    core = lax.rem(r, 2)
    chip = r // 2
    shift = shift_ref[0]
    partner = (g + 1 - 2 * odd, r)
    ahead = (lax.rem(g + 2 - 4 * odd + NG, NG), r)
    behind = (lax.rem(g - 2 + 4 * odd + NG, NG), r)
    other = (lax.rem(g - 1 + 2 * odd + NG, NG), r)
    mate = (g, r + 1 - 2 * core)
    far = (g, lax.rem(r - 1 + 2 * core + NR, NR))
    up, down = (lax.rem(g + NG - 1, NG), r), (lax.rem(g + 1, NG), r)
    left, right = (g, lax.rem(r + NR - 1, NR)), (g, lax.rem(r + 1, NR))
    chips = [(g, lax.rem(r + 2 * d, NR)) for d in range(1, 8)]
    around = [
        (a, b, (lax.rem(g + a + NG, NG), lax.rem(r + b + NR, NR)))
        for a in (-1, 0, 1) for b in (-1, 0, 1) if (a, b) != (0, 0)
    ]

    bar = pltpu.get_barrier_semaphore()
    greet = [partner, other, behind, mate, far] + chips + [t for a, b, t in around if a and b]
    for target in greet:
        pl.semaphore_signal(bar, inc=1, device_id=target, device_id_type=MESH)
    local = [
        (gs_hbm, own), (rs_hbm, rsv), (qkvw_hbm, qkvw), (bias_hbm, bias), (outw_hbm, outw),
        (blk_hbm, blk), (cs_hbm, csv), (cw_hbm, cw), (cm_hbm, cmv), (co_hbm, cov),
    ]
    loads = [pltpu.make_async_copy(a, b, lsem.at[i]) for i, (a, b) in enumerate(local)]
    for copy in loads:
        copy.start()

    def remote(src, dst, ssem, rsem, target):
        return pltpu.make_async_remote_copy(
            src_ref=src, dst_ref=dst, send_sem=ssem, recv_sem=rsem,
            device_id=target, device_id_type=MESH,
        )

    loads[0].wait()
    for i in range(8):
        sb[i] = own[i + jnp.where(i < 8 - shift, 0, 8)]
    slab[...] = jnp.zeros(slab.shape, jnp.int32)
    slab[0:1, 0:64] = src_ref[...]
    sg[chip, core] = slab[...]
    zc[:, 192:256, :] = jnp.zeros((3, 64, 256), BF16)
    pl.semaphore_wait(bar, len(greet))

    def halo_copy(c):
        start = 2 * c + odd * (6 - 4 * c)
        return remote(sb.at[pl.ds(start, 2)], pb.at[pl.ds(start, 2)], psend.at[c], precv.at[c], partner)

    def halo_in(c):
        start = 6 - 2 * c + odd * (4 * c - 6)
        return remote(sb.at[pl.ds(start, 2)], pb.at[pl.ds(start, 2)], psend.at[c], precv.at[c], partner)

    def forward_copy(c):
        if c == 3:
            at = pl.ds(1 + 5 * odd, 1)
        else:
            at = pl.ds(6 - 2 * c + odd * (4 * c - 6), 2)
        return remote(pb.at[at], fb.at[at], fsend.at[c], frecv.at[c], ahead)

    sends = [halo_copy(c) for c in range(4)]
    for copy in sends:
        copy.start()
    mate_slab = remote(slab, sg.at[chip, core], gsend.at[0], grecv.at[0], mate)
    mate_slab.start()
    sends.append(mate_slab)
    forwards = [forward_copy(c) for c in range(4)]

    def forward(c):
        halo_in(c).wait_recv()
        forwards[c].start()

    loads[1].wait()
    st32[0:1584, :] = rsv[...].reshape(1584, 128).astype(F32)
    st32[1584:2048, :] = jnp.zeros((464, 128), F32)

    def turn(y, _):
        cells = st32[pl.ds(y, 128, stride=16), :].T
        xf[pl.ds(pl.multiple_of(y * PITCH + LEAD, 8), 128), :] = cells
        at = pl.ds(pl.multiple_of(y * 8, 8), 8)
        edge[0, at, :] = cells[0:8]
        edge[1, at, :] = cells[120:128]
        return 0

    lax.fori_loop(0, 16, turn, 0)
    el[...] = edge[0].astype(BF16)
    er[...] = edge[1].astype(BF16)
    edges = [
        remote(el, rr, esend.at[0], erecv.at[0], left),
        remote(er, rl, esend.at[1], erecv.at[1], right),
    ]
    for copy in edges:
        copy.start()
    sends += edges

    mate_slab.wait_recv()
    slabs = [
        remote(sg.at[chip], sg.at[chip], gsend.at[1 + i], grecv.at[1 + i], t) for i, t in enumerate(chips)
    ]
    for copy in slabs:
        copy.start()
    sends += slabs
    forward(0)

    lanes = lax.broadcasted_iota(jnp.int32, (128, 128), 1)
    low = lanes < 64
    key_row = lax.broadcasted_iota(jnp.int32, (1, 128), 1) // 16

    def place(j, row):
        for w in range(4):
            xs[w * 128 + j * 16 : w * 128 + j * 16 + 16, :] = row[w * 16 : w * 16 + 16, :]

    def attend(k):
        def norm(w, _):
            at = pl.ds(pl.multiple_of(w * 128, 128), 128)
            values = xs[at, :].astype(F32)
            center = values - jnp.mean(values, axis=-1, keepdims=True)
            spread = jnp.mean(center * center, axis=-1, keepdims=True)
            xn[at, :] = (center * lax.rsqrt(spread + 1e-05) * gain_ref[...]).astype(BF16)
            return 0

        lax.fori_loop(0, 4, norm, 0)
        qkv[:, 0:512] = (dot(xn[...], qkvw[:, 0:512]).astype(BF16) * 0.125).astype(BF16)
        qkv[:, 512:1024] = dot(xn[...], qkvw[:, 512:1024]).astype(BF16)
        qkv[:, 1024:1536] = dot(xn[...], qkvw[:, 1024:1536]).astype(BF16)
        row_id = 16 * g - shift + 8 * k + key_row
        absent = jnp.where((row_id >= 0) & (row_id < 16 * NG), 0.0, -jnp.inf).astype(F32)
        ones = jnp.ones((128, 128), BF16)

        def window(w, _):
            at = pl.ds(pl.multiple_of(w * 128, 128), 128)
            for hp in range(4):
                q = qkv[at, hp * 128 : hp * 128 + 128]
                key = qkv[at, 512 + hp * 128 : 512 + hp * 128 + 128]
                val = qkv[at, 1024 + hp * 128 : 1024 + hp * 128 + 128]
                zero = jnp.zeros_like(q)
                q2 = jnp.concatenate([jnp.where(low, q, zero), jnp.where(low, zero, q)], axis=0)
                scores = dot_nt(q2, key) + bias[2 * hp : 2 * hp + 2].reshape(256, 128) + absent
                peak = jnp.max(scores, axis=-1, keepdims=True)
                weight = jnp.exp(scores - peak).astype(BF16)
                both = dot(weight, jnp.concatenate([val, ones], axis=1))
                out = both[:, 0:128] / both[:, 128:256]
                mixed[at, hp * 128 : hp * 128 + 128] = jnp.where(low, out[0:128], out[128:256]).astype(BF16)
            return 0

        lax.fori_loop(0, 4, window, 0)
        update = dot(mixed[...], outw[...])
        result = (xs[...].astype(F32) + update).astype(BF16)
        for w in range(4):
            for j in range(8):
                span[8 * k + j, w * 16 : w * 16 + 16, :] = result[w * 128 + j * 16 : w * 128 + j * 16 + 16]

    loads[2].wait()
    loads[3].wait()
    loads[4].wait()
    for j in range(8):
        place(j, own[8 - shift + j])
    attend(1)
    forward(1)

    for i in range(5, 10):
        loads[i].wait()
    for o in range(9):
        w1[:, o * 128 : o * 128 + 128] = jnp.concatenate([csv[o], jnp.zeros((256, 29), BF16)], axis=1)
        w2[:, o * 256 : o * 256 + 256] = cmv[o]
        a, b = o // 3, o % 3
        w3[b * 128 : b * 128 + 128, a * 256 : a * 256 + 256] = jnp.concatenate(
            [cov[o].astype(F32), jnp.zeros((29, 256), F32)], axis=0
        ).astype(BF16)

    def interpolation(y, _):
        part = blk[:, pl.ds(pl.multiple_of(y * 128, 128), 128)].astype(F32)
        cells = jnp.concatenate([part, jnp.zeros((64, 128), F32)], axis=0).T
        main = jnp.concatenate(
            [pltpu.roll(cells[120:128], 64, 1), cells, jnp.zeros((8, 128), F32)], axis=0
        )
        side = jnp.concatenate([jnp.zeros((136, 128), F32), cells[0:8]], axis=0)
        amat[rows_at(y * PITCH, PITCH), :] = jnp.concatenate([main, side], axis=1).astype(BF16)
        return 0

    lax.fori_loop(0, 16, interpolation, 0)
    forward(2)

    for copy in edges:
        copy.wait_recv()
    edge[0] = jnp.where(r > 0, rl[...].astype(F32), 0.0)
    edge[1] = jnp.where(r < NR - 1, rr[...].astype(F32), 0.0)

    def spread3(cells):
        width = cells.shape[0]
        return jnp.concatenate([pltpu.roll(cells, 1, 0), cells, pltpu.roll(cells, width - 1, 0)], axis=1).astype(BF16)

    def frame(y, _):
        at = pl.ds(pl.multiple_of(y * 8, 8), 8)
        main = xf[pl.ds(pl.multiple_of(y * PITCH + LEAD, 8), 128), :]
        cells = jnp.concatenate([edge[0, at, :], main, edge[1, at, :]], axis=0)
        x3[rows_at((y + 3) * PITCH, PITCH), :] = spread3(cells)
        return 0

    lax.fori_loop(0, 16, frame, 0)
    borders = [
        remote(x3.at[pl.ds(3 * PITCH, 3 * PITCH), pl.ds(128, 128)], hd, hsend.at[0], hrecv.at[0], up),
        remote(x3.at[pl.ds(16 * PITCH, 3 * PITCH), pl.ds(128, 128)], hu, hsend.at[1], hrecv.at[1], down),
    ]
    for copy in borders:
        copy.start()
    sends += borders
    forward(3)

    def first_conv(y0, count):
        parts = [x3[rows_at((y0 + a) * PITCH, count * PITCH), :] for a in range(3)]
        p1[rows_at(y0 * PITCH, count * PITCH), :] = dot_nt(jnp.concatenate(parts, axis=1), w1[...])

    lax.fori_loop(0, 2, lambda i, _: (first_conv(3 + 7 * i, 7), 0)[1], 0)

    for copy in slabs:
        copy.wait_recv()
    ids = sg[...].reshape(128, 128)[0:128]
    ids = jnp.concatenate([ids[8 * j : 8 * j + 1] for j in range(16)], axis=0)
    row = lax.shift_right_logical(ids, 10) - 16 * g
    col = jnp.bitwise_and(ids, 1023) - 64 * r
    token = jnp.where((col >= 0) & (col < 64), row * 64 + col, -1).astype(F32)
    token = jnp.concatenate([token, jnp.zeros((112, 128), F32)], axis=0).T
    position = lax.broadcasted_iota(jnp.int32, (64, 1024), 1).astype(F32)
    for j in range(16):
        hit = token[0:64, j : j + 1] == position
        sel[j % 2, (j // 2) * 64 : (j // 2) * 64 + 64, :] = jnp.where(hit, 1.0, 0.0).astype(BF16)
    slots = lax.broadcasted_iota(jnp.int32, (64, 64), 0)
    perm = jnp.where(slots == bid_ref[...], 1.0, 0.0).astype(BF16)

    def cross(k, halo):
        below = k // 2
        for j in range(8):
            mine = below * (16 - shift + j) + (1 - below) * (j - shift)
            theirs = below * (j - shift) + (1 - below) * (8 - shift + j)
            inside = jnp.where(below == 1, j < shift, j >= shift)
            a = own[jnp.clip(mine, 0, 15)]
            b = halo[jnp.clip(theirs, 0, 7)]
            place(j, jnp.where(inside, a, b))
        attend(k)

    cross(2 - 2 * odd, pb)
    for copy in forwards:
        copy.wait_recv()
    cross(2 * odd, fb)

    for i in range(16):
        onext[i] = span[shift + i]
    store_g = pltpu.make_async_copy(onext, gnext_hbm, osem.at[0])
    store_g.start()
    yv[...] = dot_nt(onext[...].reshape(1024, 512), cw[...]).astype(BF16)
    zs[1 - core] = dot(sel[1 - core], yv[...]).astype(BF16)
    to_mate = remote(zs.at[1 - core], zr, asend, arecv, mate)
    to_mate.start()
    zs[core] = dot(sel[core], yv[...]).astype(BF16)
    to_mate.wait()
    zs[core] = zs[core] + zr[...]
    tiles = []
    for i, t in enumerate(chips):
        q = lax.rem(chip + i + 1, 8)
        tiles.append(remote(zs.at[core, rows_at(q * 64, 64)], z2.at[i], bsend.at[i], brecv.at[i], t))
    for copy in tiles:
        copy.start()
    for copy in borders:
        copy.wait_recv()
    for a in range(3):
        at = pl.ds(a * PITCH, PITCH)
        x3[a * PITCH : (a + 1) * PITCH, :] = spread3(jnp.where(g > 0, hu[at, :].astype(F32), 0.0))
        x3[(19 + a) * PITCH : (20 + a) * PITCH, :] = spread3(jnp.where(g < NG - 1, hd[at, :].astype(F32), 0.0))
    lax.fori_loop(0, 2, lambda i, _: (first_conv(17 * i, 3), 0)[1], 0)
    total = zs[core, rows_at(chip * 64, 64), :].astype(F32)
    for copy in tiles:
        copy.wait()
    for i in range(7):
        total = total + z2[i].astype(F32)
    zc[1, 0:64, :] = dot(perm, total.astype(BF16)).astype(BF16)
    ring = []
    for i, (a, b, t) in enumerate(around):
        at = pl.ds((0, 64, 128)[b], 64)
        ring.append(remote(zc.at[1, pl.ds(0, 64)], zc.at[1 - a, at], nsend.at[i], nrecv.at[i], t))
    for copy in ring:
        copy.start()
    sends += ring
    for copy in ring:
        copy.wait_recv()

    cell = lax.broadcasted_iota(jnp.int32, (PITCH, 256), 0)
    across = ((cell >= LEAD) | (r > 0)) & ((cell < LEAD + 128) | (r < NR - 1))

    def on_grid(values, y):
        here = 16 * g + y
        return jnp.where(across & (here >= 0) & (here < 16 * NG), values, 0.0)

    def first_hidden(y0, a0, count, band):
        size = count * PITCH
        u = p1[rows_at((y0 + 2) * PITCH, size), :] + dot(amat[rows_at(a0 * PITCH, size), :], zc[band])
        u = silu(u)
        for i in range(count):
            cells = on_grid(u[i * PITCH : (i + 1) * PITCH], y0 + i)
            xm[rows_at((y0 + 2 + i) * PITCH, PITCH), :] = spread3(cells)

    lax.fori_loop(0, 4, lambda i, _: (first_hidden(4 * i, 4 * i, 4, 1), 0)[1], 0)
    first_hidden(-2, 14, 2, 0)
    first_hidden(16, 0, 2, 2)

    def second_hidden(i, _):
        y0 = 3 * i
        parts = [xm[rows_at((y0 + a) * PITCH, 3 * PITCH), :] for a in range(3)]
        u = silu(dot_nt(jnp.concatenate(parts, axis=1), w2[...]))
        for j in range(3):
            cells = on_grid(u[j * PITCH : (j + 1) * PITCH], y0 + j - 1)
            x2[rows_at((y0 + j) * PITCH, PITCH), :] = cells.astype(BF16)
        return 0

    lax.fori_loop(0, 6, second_hidden, 0)

    def last_conv(i, _):
        y0 = 4 * i
        parts = [x2[rows_at((y0 + a) * PITCH, 4 * PITCH), :] for a in range(3)]
        terms = dot_nt(jnp.concatenate(parts, axis=1), w3[...])
        for j in range(4):
            t = terms[j * PITCH : (j + 1) * PITCH]
            total = pltpu.roll(t[:, 0:128], 1, 0) + t[:, 128:256] + pltpu.roll(t[:, 256:384], PITCH - 1, 0)
            at = pl.ds(y0 + j, 128, stride=16)
            ost[at, :] = st32[at, :] + total[LEAD : LEAD + 128].T
        return 0

    lax.fori_loop(0, 4, last_conv, 0)
    store_r = pltpu.make_async_copy(ost.at[pl.ds(0, 1584)], rnext_hbm, osem.at[1])
    store_r.start()
    for copy in sends + forwards:
        copy.wait_send()
    store_g.wait()
    store_r.wait()


def on_device(
    global_state, norm_gain, qkv_weight, out_weight, position_bias, regional_state,
    conv_state, cond_weight, conv_mid, conv_out, blocks, sources, block_ids, shift_offset,
):
    vm, anywhere = pl.BlockSpec(memory_space=pltpu.VMEM), pl.BlockSpec(memory_space=pl.ANY)
    dma = pltpu.SemaphoreType.DMA
    scratch = [
        ((16, 64, 512), BF16), ((99, 16, 128), BF16), ((512, 1536), BF16), ((512, 512), BF16),
        ((8, 128, 128), F32), ((9, 256, 99), BF16), ((256, 512), BF16), ((9, 256, 256), BF16),
        ((9, 99, 256), BF16), ((64, 2048), BF16),
        ((8, 64, 512), BF16), ((8, 64, 512), BF16), ((8, 64, 512), BF16),
        ((8, 128), jnp.int32), ((8, 2, 8, 128), jnp.int32),
        ((512, 512), BF16), ((512, 512), BF16), ((512, 1536), BF16), ((512, 512), BF16),
        ((24, 64, 512), BF16), ((16, 64, 512), BF16), ((1024, 256), BF16),
        ((2, 512, 1024), BF16), ((2, 512, 256), BF16), ((512, 256), BF16),
        ((7, 64, 256), BF16), ((3, 256, 256), BF16),
        ((2048, 128), F32), ((2, 128, 128), F32),
        ((128, 128), BF16), ((128, 128), BF16), ((128, 128), BF16), ((128, 128), BF16),
        ((16 * PITCH, 128), F32), ((22 * PITCH, 384), BF16),
        ((3 * PITCH, 128), BF16), ((3 * PITCH, 128), BF16), ((20 * PITCH, 256), F32),
        ((256, 1152), BF16), ((256, 2304), BF16), ((384, 768), BF16),
        ((16 * PITCH, 256), BF16), ((20 * PITCH, 768), BF16), ((18 * PITCH, 256), BF16),
        ((2048, 128), F32),
    ]
    counts = [10, 4, 4, 4, 4, 2, 2, 2, 2, 8, 8, 0, 0, 7, 7, 8, 8, 2]
    gnext, rnext = pl.pallas_call(
        body,
        out_shape=[
            jax.ShapeDtypeStruct((16, 64, 512), BF16),
            jax.ShapeDtypeStruct((1584, 128), F32),
        ],
        in_specs=[pl.BlockSpec(memory_space=pltpu.SMEM)] + [vm] * 3 + [anywhere] * 10,
        out_specs=[anywhere, anywhere],
        scratch_shapes=[pltpu.VMEM(*s) for s in scratch] + [dma((n,)) if n else dma for n in counts],
        compiler_params=pltpu.CompilerParams(
            collective_id=0, has_side_effects=True, vmem_limit_bytes=60 * 2**20
        ),
    )(
        shift_offset, sources.reshape(1, 64), block_ids.reshape(1, 64), norm_gain.reshape(1, 512),
        global_state, regional_state, qkv_weight, out_weight, position_bias,
        conv_state, cond_weight, conv_mid, conv_out, blocks,
    )
    return gnext, rnext.reshape(99, 16, 128)


def solution(mesh):
    return jax.shard_map(
        on_device,
        mesh=mesh,
        in_specs=(
            P("glob", "reg", None),
            P(), P(), P(), P(),
            P(None, "glob", "reg"),
            P(), P(), P(), P(), P(),
            P("glob", "reg", None),
            P("glob", "reg", None),
            P(),
        ),
        out_specs=(P("glob", "reg", None), P(None, "glob", "reg")),
        check_vma=False,
    )
```

```python
import jax
import jax.numpy as jnp
from jax import lax
from jax.experimental import pallas as pl
from jax.experimental.pallas import tpu as pltpu
from jax.sharding import PartitionSpec as P

MESH = pl.DeviceIdType.MESH
F32 = jnp.float32
BF16 = jnp.bfloat16
NG, NR = 8, 16
PITCH, LEAD = 144, 8
NT = (((1,), (1,)), ((), ()))


def dot(a, b):
    return jnp.dot(a, b, preferred_element_type=F32)


def dot_nt(a, b):
    return lax.dot_general(a, b, NT, preferred_element_type=F32)


def silu(u):
    half = 0.5 * u
    return half + half * jnp.tanh(half)


def rows_at(index, count):
    return pl.ds(pl.multiple_of(index, 16), count)


def body(
    shift_ref, src_ref, bid_ref, gain_ref,
    gs_hbm, rs_hbm, qkvw_hbm, outw_hbm, bias_hbm, cs_hbm, cw_hbm, cm_hbm, co_hbm, blk_hbm,
    gnext_hbm, rnext_hbm,
    own, rsv, qkvw, outw, bias, csv, cw, cmv, cov, blk,
    sb, pb, fb, xb, hb, slab, sg, xn, qk, qkv, qp, kv, biasr, span, packed, onext, yv, sel, zpart, zs, zr, z2, zc, cout, cin,
    st32, edge, el, er, rl, rr, xf, x3, hu, hd, p1, w1, w2, w3, amat, xm, x2, pt, ost,
    lsem, psend, precv, fsend, frecv, esend, erecv, hsend, hrecv, gsend, grecv,
    asend, arecv, bsend, brecv, nsend, nrecv, osem,
):
    g = lax.axis_index("glob")
    r = lax.axis_index("reg")
    odd = lax.rem(g, 2)
    core = lax.rem(r, 2)
    chip = r // 2
    shift = shift_ref[0]
    partner = (g + 1 - 2 * odd, r)
    ahead = (lax.rem(g + 2 - 4 * odd + NG, NG), r)
    behind = (lax.rem(g - 2 + 4 * odd + NG, NG), r)
    other = (lax.rem(g - 1 + 2 * odd + NG, NG), r)
    mate = (g, r + 1 - 2 * core)
    far = (g, lax.rem(r - 1 + 2 * core + NR, NR))
    up, down = (lax.rem(g + NG - 1, NG), r), (lax.rem(g + 1, NG), r)
    left, right = (g, lax.rem(r + NR - 1, NR)), (g, lax.rem(r + 1, NR))
    chips = [(g, lax.rem(r + 2 * d, NR)) for d in range(1, 8)]
    around = [
        (a, b, (lax.rem(g + a + NG, NG), lax.rem(r + b + NR, NR)))
        for a in (-1, 0, 1) for b in (-1, 0, 1) if (a, b) != (0, 0)
    ]

    bar = pltpu.get_barrier_semaphore()
    greet = [partner, other, ahead, behind, mate, far] + chips + [t for a, b, t in around if a and b]
    for target in greet:
        pl.semaphore_signal(bar, inc=1, device_id=target, device_id_type=MESH)
    local = [
        (gs_hbm, own), (rs_hbm, rsv), (qkvw_hbm, qkvw), (bias_hbm, bias), (outw_hbm, outw),
        (blk_hbm, blk), (cs_hbm, csv), (cw_hbm, cw), (cm_hbm, cmv), (co_hbm, cov),
    ]
    loads = [pltpu.make_async_copy(a, b, lsem.at[i]) for i, (a, b) in enumerate(local)]
    for copy in loads:
        copy.start()

    def remote(src, dst, ssem, rsem, target):
        return pltpu.make_async_remote_copy(
            src_ref=src, dst_ref=dst, send_sem=ssem, recv_sem=rsem,
            device_id=target, device_id_type=MESH,
        )

    loads[0].wait()
    for i in range(4):
        sb[i] = own[i + jnp.where(i < 8 - shift, 0, 8)]
    slab[...] = jnp.zeros(slab.shape, jnp.int32)
    slab[0:1, 0:64] = src_ref[...]
    sg[chip, core] = slab[...]
    zc[1, 192:256, :] = jnp.zeros((64, 256), BF16)
    for band in (0, 2):
        zc[band, 64:256, :] = jnp.zeros((192, 256), BF16)
    pl.semaphore_wait(bar, len(greet))

    firsts, seconds, forwards, mergeds = [], [], [], []
    for c in range(2):
        at, late = pl.ds(2 * c, 2), pl.ds(4 + 2 * c, 2)
        firsts.append(remote(sb.at[at], pb.at[at], psend.at[c], precv.at[c], partner))
        seconds.append(remote(own.at[pl.ds(4 + 2 * c + 8 * odd, 2)], xb.at[at], psend.at[2 + c], precv.at[2 + c], behind))
        forwards.append(remote(pb.at[at], fb.at[at], fsend.at[c], frecv.at[c], ahead))
        mergeds.append(remote(sb.at[late], hb.at[late], fsend.at[2 + c], frecv.at[2 + c], partner))
    for c in range(2):
        firsts[c].start()
        seconds[c].start()
    mate_slab = remote(slab, sg.at[chip, core], gsend.at[0], grecv.at[0], mate)
    mate_slab.start()
    sends = firsts + seconds + forwards + mergeds + [mate_slab]

    def pass_on(c):
        firsts[c].wait_recv()
        forwards[c].start()
        seconds[c].wait_recv()
        for i in range(4 + 2 * c, 6 + 2 * c):
            for_partner = own[i + 8 * (1 - odd)]
            from_behind = xb[i - 4]
            up_row = i < 8 - shift
            sb[i] = jnp.where(jnp.where(odd == 1, jnp.logical_not(up_row), up_row), from_behind, for_partner)
        mergeds[c].start()

    loads[1].wait()
    st32[0:1584, :] = rsv[...].reshape(1584, 128).astype(F32)
    st32[1584:2048, :] = jnp.zeros((464, 128), F32)

    def turn(y, _):
        cells = st32[pl.ds(y, 128, stride=16), :].T
        xf[pl.ds(pl.multiple_of(y * PITCH + LEAD, 8), 128), :] = cells
        at = pl.ds(pl.multiple_of(y * 8, 8), 8)
        edge[0, at, :] = cells[0:8]
        edge[1, at, :] = cells[120:128]
        return 0

    lax.fori_loop(0, 16, turn, 0, unroll=True)
    el[...] = edge[0].astype(BF16)
    er[...] = edge[1].astype(BF16)
    edges = [
        remote(el, rr, esend.at[0], erecv.at[0], left),
        remote(er, rl, esend.at[1], erecv.at[1], right),
    ]
    for copy in edges:
        copy.start()
    sends += edges

    mate_slab.wait_recv()
    slabs = [
        remote(sg.at[chip], sg.at[chip], gsend.at[1 + i], grecv.at[1 + i], t) for i, t in enumerate(chips)
    ]
    for copy in slabs:
        copy.start()
    sends += slabs

    low = lax.broadcasted_iota(jnp.int32, (128, 128), 1) < 64
    upward = [i < 8 - shift for i in range(8)]
    packed_row = [i + jnp.where(upward[i], 0, 8) for i in range(8)]

    def project(tokens, at, first):
        count = tokens.shape[0] * 64
        for w in range(0, count, 128):
            values = tokens[w // 64 : w // 64 + 2].reshape(128, 512).astype(F32)
            center = values - jnp.mean(values, axis=-1, keepdims=True)
            spread = jnp.mean(center * center, axis=-1, keepdims=True)
            xn[w : w + 128, :] = (center * lax.rsqrt(spread + 1e-05) * gain_ref[...]).astype(BF16)
        for n in range(first, 3):
            part = dot(xn[0:count, :], qkvw[:, n * 512 : n * 512 + 512]).astype(BF16)
            if n == 0:
                part = (part * 0.125).astype(BF16)
            qk[at : at + count // 64, :, n * 512 : n * 512 + 512] = part.reshape(count // 64, 64, 512)

    places = [(w, hp) for w in range(4) for hp in range(4)]

    def two_heads(q):
        zero = jnp.zeros_like(q)
        return jnp.concatenate([jnp.where(low, q, zero), jnp.where(low, zero, q)], axis=0)

    def keep(w, hp, mixed):
        for j in range(8):
            span[j, w * 16 : w * 16 + 16, hp * 128 : hp * 128 + 128] = mixed[j * 16 : j * 16 + 16]

    def attend_inner():
        for j in range(8):
            row = qk[8 - shift + j]
            for w in range(4):
                qkv[w * 128 + j * 16 : w * 128 + j * 16 + 16, :] = row[w * 16 : w * 16 + 16, :]
        ones = jnp.ones((128, 128), BF16)
        scores = []
        for w, hp in places:
            q = qkv[w * 128 : w * 128 + 128, hp * 128 : hp * 128 + 128]
            key = qkv[w * 128 : w * 128 + 128, 512 + hp * 128 : 512 + hp * 128 + 128]
            scores.append(dot_nt(two_heads(q), key))
        weights = []
        for (w, hp), score in zip(places, scores):
            score = score + bias[2 * hp : 2 * hp + 2].reshape(256, 128)
            weights.append(jnp.exp(score - jnp.max(score, axis=-1, keepdims=True)).astype(BF16))
        sums = []
        for (w, hp), weight in zip(places, weights):
            val = qkv[w * 128 : w * 128 + 128, 1024 + hp * 128 : 1024 + hp * 128 + 128]
            sums.append(dot(weight, jnp.concatenate([val, ones], axis=1)))
        for (w, hp), both in zip(places, sums):
            top = jnp.where(low, both[0:128, 0:128], both[128:256, 0:128])
            under = jnp.where(low, both[0:128, 128:256], both[128:256, 128:256])
            keep(w, hp, (top / under).astype(BF16))

    def cross_setup():
        for i in range(8):
            row = qk[packed_row[i], :, 0:512]
            for w in range(4):
                qp[w * 128 + i * 16 : w * 128 + i * 16 + 16, :] = row[w * 16 : w * 16 + 16, :]
        first = lax.broadcasted_iota(jnp.int32, (16, 128), 1) // 16 < shift
        for i in range(8):
            above = jnp.where((g == 0) & first, -jnp.inf, 0.0)
            below = jnp.where((g < NG - 1) | first, 0.0, -jnp.inf)
            absent = jnp.where(upward[i], above, below).astype(F32)
            at = i + shift - jnp.where(i + shift >= 8, 8, 0)
            for h in range(8):
                biasr[h, i * 16 : i * 16 + 16, :] = bias[h, at] + absent

    def attend_cross():
        for j in range(8):
            rows = (
                qk[jnp.where(j < shift, 24 - shift + j, j - shift), :, 512:1536],
                qk[jnp.where(j < shift, 16 - shift + j, 16 + j - shift), :, 512:1536],
            )
            for k in range(2):
                for w in range(4):
                    at = w * 256 + k * 128 + j * 16
                    kv[at : at + 16, :] = rows[k][w * 16 : w * 16 + 16, :]
        upper = (lax.broadcasted_iota(jnp.int32, (256, 128), 0) // 16) % 8 < 8 - shift
        scores = []
        for w, hp in places:
            q = qp[w * 128 : w * 128 + 128, hp * 128 : hp * 128 + 128]
            scores.append(dot_nt(two_heads(q), kv[w * 256 : w * 256 + 256, hp * 128 : hp * 128 + 128]))
        weights, sums = [], []
        for (w, hp), score in zip(places, scores):
            score = jnp.where(upper, score[:, 0:128], score[:, 128:256])
            score = score + biasr[2 * hp : 2 * hp + 2].reshape(256, 128)
            weight = jnp.exp(score - jnp.max(score, axis=-1, keepdims=True))
            sums.append(jnp.sum(weight, axis=-1, keepdims=True))
            weights.append(weight.astype(BF16))
        mixes = []
        for (w, hp), weight in zip(places, weights):
            cols = slice(512 + hp * 128, 512 + hp * 128 + 128)
            vals = [kv[w * 256 + k * 128 : w * 256 + k * 128 + 128, cols] for k in range(2)]
            mixes.append(dot(weight, jnp.concatenate(vals, axis=1)))
        for (w, hp), mix, total in zip(places, mixes, sums):
            mix = jnp.where(upper, mix[:, 0:128], mix[:, 128:256]) / total
            keep(w, hp, jnp.where(low, mix[0:128], mix[128:256]).astype(BF16))

    def update(at, index):
        change = dot(span[...].reshape(512, 512), outw[...])
        for i in range(8):
            mine = own[index(i)].astype(F32) + change[i * 64 : i * 64 + 64]
            packed[at + i] = mine.astype(BF16)
        tokens = packed[at : at + 8].reshape(512, 512)
        yv[at * 64 : at * 64 + 512, :] = dot_nt(tokens, cw[...]).astype(BF16)

    loads[2].wait()
    project(own[...], 0, 0)
    pass_on(0)
    for i in range(3, 10):
        loads[i].wait()
    attend_inner()
    update(8, lambda j: 8 - shift + j)
    cross_setup()

    for o in range(9):
        w1[o * 128 : o * 128 + 128, :] = jnp.concatenate(
            [csv[o].astype(F32), jnp.zeros((29, 256), F32)], axis=0
        ).astype(BF16)
        w2[:, o * 256 : o * 256 + 256] = cmv[o]
        a, b = o // 3, o % 3
        w3[b * 128 : b * 128 + 128, a * 256 : a * 256 + 256] = jnp.concatenate(
            [cov[o].astype(F32), jnp.zeros((29, 256), F32)], axis=0
        ).astype(BF16)

    def interpolation(y, _):
        part = blk[:, pl.ds(pl.multiple_of(y * 128, 128), 128)].astype(F32)
        cells = jnp.concatenate([part, jnp.zeros((64, 128), F32)], axis=0).T
        main = jnp.concatenate(
            [pltpu.roll(cells[120:128], 64, 1), cells, jnp.zeros((8, 128), F32)], axis=0
        )
        side = jnp.concatenate([jnp.zeros((136, 128), F32), cells[0:8]], axis=0)
        amat[rows_at(y * PITCH, PITCH), :] = jnp.concatenate([main, side], axis=1).astype(BF16)
        return 0

    lax.fori_loop(0, 16, interpolation, 0, unroll=True)
    pass_on(1)

    for copy in edges:
        copy.wait_recv()
    edge[0] = jnp.where(r > 0, rl[...].astype(F32), 0.0)
    edge[1] = jnp.where(r < NR - 1, rr[...].astype(F32), 0.0)

    def spread3(cells):
        width = cells.shape[0]
        return jnp.concatenate([pltpu.roll(cells, 1, 0), cells, pltpu.roll(cells, width - 1, 0)], axis=1).astype(BF16)

    def frame(y, _):
        at = pl.ds(pl.multiple_of(y * 8, 8), 8)
        main = xf[pl.ds(pl.multiple_of(y * PITCH + LEAD, 8), 128), :]
        cells = jnp.concatenate([edge[0, at, :], main, edge[1, at, :]], axis=0)
        x3[rows_at((y + 3) * PITCH, PITCH), :] = spread3(cells)
        return 0

    lax.fori_loop(0, 16, frame, 0, unroll=True)
    borders = [
        remote(x3.at[pl.ds(3 * PITCH, 3 * PITCH), pl.ds(128, 128)], hd, hsend.at[0], hrecv.at[0], up),
        remote(x3.at[pl.ds(16 * PITCH, 3 * PITCH), pl.ds(128, 128)], hu, hsend.at[1], hrecv.at[1], down),
    ]

    def first_conv(y0, count):
        parts = [x3[rows_at((y0 + a) * PITCH, count * PITCH), :] for a in range(3)]
        p1[rows_at(y0 * PITCH, count * PITCH), :] = dot(jnp.concatenate(parts, axis=1), w1[...])

    lax.fori_loop(0, 2, lambda i, _: (first_conv(3 + 7 * i, 7), 0)[1], 0, unroll=True)

    for copy in slabs:
        copy.wait_recv()
    ids = sg[...].reshape(128, 128)[0:128]
    ids = jnp.concatenate([ids[8 * j : 8 * j + 1] for j in range(16)], axis=0)
    row = lax.shift_right_logical(ids, 10) - 16 * g
    col = jnp.bitwise_and(ids, 1023) - 64 * r
    row = jnp.where(row < 8 - shift, row, jnp.where(row >= 16 - shift, row - 8, row + shift))
    token = jnp.where((col >= 0) & (col < 64), row * 64 + col, -1).astype(F32)
    token = jnp.concatenate([token, jnp.zeros((112, 128), F32)], axis=0).T
    position = lax.broadcasted_iota(jnp.int32, (64, 1024), 1).astype(F32)
    for j in range(16):
        hit = token[0:64, j : j + 1] == position
        sel[j % 2, (j // 2) * 64 : (j // 2) * 64 + 64, :] = jnp.where(hit, 1.0, 0.0).astype(BF16)
    for half in range(2):
        zpart[half] = dot(sel[half, :, 512:1024], yv[512:1024, :])
    slots = lax.broadcasted_iota(jnp.int32, (64, 64), 0)
    perm = jnp.where(slots == bid_ref[...], 1.0, 0.0).astype(BF16)

    for copy in forwards + mergeds:
        copy.wait_recv()
    for copy in borders:
        copy.start()
    sends += borders
    for i in range(4):
        hb[i] = jnp.where(jnp.where(odd == 1, upward[i], jnp.logical_not(upward[i])), fb[i], pb[i])
    project(hb[...], 16, 1)
    attend_cross()

    update(0, lambda i: packed_row[i])

    def contribution(half):
        zs[half] = (zpart[half] + dot(sel[half, :, 0:512], yv[0:512, :])).astype(BF16)

    contribution(1 - core)
    to_mate = remote(zs.at[1 - core], zr, asend, arecv, mate)
    to_mate.start()
    contribution(core)
    for i in range(16):
        onext[i] = packed[jnp.where(i < 8 - shift, i, jnp.where(i >= 16 - shift, i - 8, i + shift))]
    store_g = pltpu.make_async_copy(onext, gnext_hbm, osem.at[0])
    store_g.start()
    to_mate.wait()
    zs[core] = zs[core] + zr[...]
    tiles = []
    for i, t in enumerate(chips):
        q = lax.rem(chip + i + 1, 8)
        tiles.append(remote(zs.at[core, rows_at(q * 64, 64)], z2.at[i], bsend.at[i], brecv.at[i], t))
    for copy in tiles:
        copy.start()
    for copy in borders:
        copy.wait_recv()
    for a in range(3):
        at = pl.ds(a * PITCH, PITCH)
        x3[a * PITCH : (a + 1) * PITCH, :] = spread3(jnp.where(g > 0, hu[at, :].astype(F32), 0.0))
        x3[(19 + a) * PITCH : (20 + a) * PITCH, :] = spread3(jnp.where(g < NG - 1, hd[at, :].astype(F32), 0.0))
    lax.fori_loop(0, 2, lambda i, _: (first_conv(17 * i, 3), 0)[1], 0, unroll=True)
    total = zs[core, rows_at(chip * 64, 64), :].astype(F32)
    for copy in tiles:
        copy.wait()
    for i in range(7):
        total = total + z2[i].astype(F32)
    zc[1, 0:64, :] = dot(perm, total.astype(BF16)).astype(BF16)
    corner_rows = [amat[y * PITCH + at : y * PITCH + at + 16, 0:64] for y in (0, 1, 14, 15) for at in (0, PITCH - 16)]
    corners = dot(jnp.concatenate(corner_rows, axis=0), zc[1, 0:64])
    for i in range(4):
        at = [(4 * (i // 2) + 2 * n + i % 2) * 16 + 8 * (1 - i % 2) for n in range(2)]
        cout[i] = jnp.concatenate([corners[at[0] : at[0] + 8], corners[at[1] : at[1] + 8]], axis=0).astype(BF16)
    ring = []
    for i, (a, b, t) in enumerate(around):
        if a and b:
            here, there = (1 + a) + (1 + b) // 2, (1 - a) + (1 - b) // 2
            ring.append(remote(cout.at[here], cin.at[there], nsend.at[i], nrecv.at[i], t))
        else:
            at = pl.ds((0, 64, 128)[b], 64)
            ring.append(remote(zc.at[1, pl.ds(0, 64)], zc.at[1 - a, at], nsend.at[i], nrecv.at[i], t))
    for copy in ring:
        copy.start()
    sends += ring

    cell = lax.broadcasted_iota(jnp.int32, (PITCH, 256), 0)
    across = ((cell >= LEAD) | (r > 0)) & ((cell < LEAD + 128) | (r < NR - 1))

    def on_grid(values, y):
        here = 16 * g + y
        return jnp.where(across & (here >= 0) & (here < 16 * NG), values, 0.0)

    for y0 in range(0, 16, 4):
        size = 4 * PITCH
        at = pl.ds(y0 * PITCH, size)
        u = p1[(y0 + 2) * PITCH : (y0 + 2) * PITCH + size, :] + dot(amat[at, 0:64], zc[1, 0:64])
        u = silu(u)
        for i in range(4):
            xm[(y0 + 2 + i) * PITCH : (y0 + 3 + i) * PITCH, :] = spread3(u[i * PITCH : (i + 1) * PITCH])

    def second_inner(y0, count):
        parts = [
            jnp.concatenate([xm[(y0 + i + a) * PITCH + 16 : (y0 + i + a) * PITCH + 128, :] for i in range(count)], axis=0)
            for a in range(3)
        ]
        u = silu(dot_nt(jnp.concatenate(parts, axis=1), w2[...])).astype(BF16)
        for i in range(count):
            x2[(y0 + i) * PITCH + 16 : (y0 + i) * PITCH + 128, :] = u[i * 112 : i * 112 + 112]

    second_inner(2, 7)
    second_inner(9, 7)

    def last_terms(cells):
        parts = [jnp.concatenate([x2[(y + a) * PITCH + p : (y + a) * PITCH + p + n, :] for y, p, n in cells], axis=0) for a in range(3)]
        terms = dot_nt(jnp.concatenate(parts, axis=1), w3[...])
        start = 0
        for y, p, n in cells:
            pt[y * PITCH + p : y * PITCH + p + n, :] = terms[start : start + n]
            start += n

    last_terms([(y, 16, 112) for y in range(2, 8)])
    last_terms([(y, 16, 112) for y in range(8, 14)])

    for copy in ring:
        copy.wait_recv()

    def first_rows(y0, a0, band):
        size = 2 * PITCH
        u = p1[(y0 + 2) * PITCH : (y0 + 2) * PITCH + size, :] + dot(amat[a0 * PITCH : a0 * PITCH + size, :], zc[band])
        ends = [cin[band + side].astype(F32) for side in range(2)]
        for i in range(2):
            cond = jnp.concatenate(
                [ends[0][8 * i : 8 * i + 8], jnp.zeros((128, 256), F32), ends[1][8 * i : 8 * i + 8]], axis=0
            )
            cells = on_grid(silu(u[i * PITCH : (i + 1) * PITCH] + cond), y0 + i)
            xm[(y0 + 2 + i) * PITCH : (y0 + 3 + i) * PITCH, :] = spread3(cells)

    first_rows(-2, 14, 0)
    first_rows(16, 0, 2)

    def edge_cells(ref, y, width):
        return [ref[y * PITCH : y * PITCH + width, :], ref[(y + 1) * PITCH - width : (y + 1) * PITCH, :]]

    own_part = jnp.concatenate([c for y in range(2, 18) for c in edge_cells(p1, y, 32)], axis=0)
    tile_part = jnp.concatenate([c for y in range(16) for c in edge_cells(amat, y, 32)], axis=0)
    u = silu(own_part + dot(tile_part, zc[1]))
    for y in range(16):
        for side in range(2):
            cells = u[(2 * y + side) * 32 : (2 * y + side) * 32 + 32]
            inside = across[0:32] if side == 0 else across[PITCH - 32 : PITCH]
            cells = spread3(jnp.where(inside, cells, 0.0))
            at = (y + 2) * PITCH + (0 if side == 0 else PITCH - 16)
            xm[at : at + 16, :] = cells[0:16] if side == 0 else cells[16:32]

    def second_rows(y0):
        parts = [xm[(y0 + a) * PITCH : (y0 + a + 2) * PITCH, :] for a in range(3)]
        u = silu(dot_nt(jnp.concatenate(parts, axis=1), w2[...]))
        for i in range(2):
            cells = on_grid(u[i * PITCH : (i + 1) * PITCH], y0 + i - 1)
            x2[(y0 + i) * PITCH : (y0 + i + 1) * PITCH, :] = cells.astype(BF16)

    second_rows(0)
    second_rows(16)
    parts = [jnp.concatenate([c for y in range(2, 16) for c in edge_cells(xm, y + a, 16)], axis=0) for a in range(3)]
    u = silu(dot_nt(jnp.concatenate(parts, axis=1), w2[...]))
    for y in range(2, 16):
        for side in range(2):
            cells = u[(y - 2) * 32 + side * 16 : (y - 2) * 32 + side * 16 + 16]
            inside = across[0:16] if side == 0 else across[PITCH - 16 : PITCH]
            at = y * PITCH + (0 if side == 0 else PITCH - 16)
            x2[at : at + 16, :] = jnp.where(inside, cells, 0.0).astype(BF16)

    last_terms([(y, 0, PITCH) for y in (0, 1, 14, 15)] + [(y, p, 16) for y in range(2, 14) for p in (0, PITCH - 16)])
    for y in range(16):
        t = pt[y * PITCH : (y + 1) * PITCH, :]
        total = pltpu.roll(t[:, 0:128], 1, 0) + t[:, 128:256] + pltpu.roll(t[:, 256:384], PITCH - 1, 0)
        at = pl.ds(y, 128, stride=16)
        ost[at, :] = st32[at, :] + total[LEAD : LEAD + 128].T
    store_r = pltpu.make_async_copy(ost.at[pl.ds(0, 1584)], rnext_hbm, osem.at[1])
    store_r.start()
    for copy in sends:
        copy.wait_send()
    store_g.wait()
    store_r.wait()


def hand_over(gnext_in, rnext_in, gnext_out, rnext_out, gbuf, rbuf, isem, osem):
    pairs = []
    for i in range(4):
        at, rows = pl.ds(4 * i, 4), pl.ds(400 * i, 400 if i < 3 else 384)
        for n, (a, b, c, part) in enumerate(((gnext_in, gbuf, gnext_out, at), (rnext_in, rbuf, rnext_out, rows))):
            first = pltpu.make_async_copy(a.at[part], b.at[part], isem.at[2 * i + n])
            pairs.append((first, pltpu.make_async_copy(b.at[part], c.at[part], osem.at[2 * i + n])))
    for first, _ in pairs:
        first.start()
    for first, second in pairs:
        first.wait()
        second.start()
    for _, second in pairs:
        second.wait()


def on_device(
    global_state, norm_gain, qkv_weight, out_weight, position_bias, regional_state,
    conv_state, cond_weight, conv_mid, conv_out, blocks, sources, block_ids, shift_offset,
):
    vm, anywhere = pl.BlockSpec(memory_space=pltpu.VMEM), pl.BlockSpec(memory_space=pl.ANY)
    dma = pltpu.SemaphoreType.DMA
    scratch = [
        ((16, 64, 512), BF16), ((99, 16, 128), BF16), ((512, 1536), BF16), ((512, 512), BF16),
        ((8, 8, 16, 128), F32), ((9, 99, 256), BF16), ((256, 512), BF16), ((9, 256, 256), BF16),
        ((9, 99, 256), BF16), ((64, 2048), BF16),
        ((8, 64, 512), BF16), ((4, 64, 512), BF16), ((4, 64, 512), BF16),
        ((4, 64, 512), BF16), ((8, 64, 512), BF16),
        ((8, 128), jnp.int32), ((8, 2, 8, 128), jnp.int32),
        ((1024, 512), BF16), ((24, 64, 1536), BF16), ((512, 1536), BF16),
        ((512, 512), BF16), ((1024, 1024), BF16), ((8, 128, 128), F32),
        ((8, 64, 512), BF16), ((16, 64, 512), BF16), ((16, 64, 512), BF16), ((1024, 256), BF16),
        ((2, 512, 1024), BF16), ((2, 512, 256), F32), ((2, 512, 256), BF16), ((512, 256), BF16),
        ((7, 64, 256), BF16), ((3, 256, 256), BF16), ((4, 16, 256), BF16), ((4, 16, 256), BF16),
        ((2048, 128), F32), ((2, 128, 128), F32),
        ((128, 128), BF16), ((128, 128), BF16), ((128, 128), BF16), ((128, 128), BF16),
        ((16 * PITCH, 128), F32), ((22 * PITCH, 384), BF16),
        ((3 * PITCH, 128), BF16), ((3 * PITCH, 128), BF16), ((20 * PITCH, 256), F32),
        ((1152, 256), BF16), ((256, 2304), BF16), ((384, 768), BF16),
        ((16 * PITCH, 256), BF16), ((20 * PITCH, 768), BF16), ((18 * PITCH, 256), BF16),
        ((16 * PITCH, 384), F32), ((2048, 128), F32),
    ]
    counts = [10, 4, 4, 4, 4, 2, 2, 2, 2, 8, 8, 0, 0, 7, 7, 8, 8, 2]
    gnext, rnext = pl.pallas_call(
        body,
        out_shape=[
            jax.ShapeDtypeStruct((16, 64, 512), BF16),
            jax.ShapeDtypeStruct((1584, 128), F32),
        ],
        in_specs=[pl.BlockSpec(memory_space=pltpu.SMEM)] + [vm] * 3 + [anywhere] * 10,
        out_specs=[anywhere, anywhere],
        scratch_shapes=[pltpu.VMEM(*s) for s in scratch] + [dma((n,)) if n else dma for n in counts],
        compiler_params=pltpu.CompilerParams(
            collective_id=0, has_side_effects=True, vmem_limit_bytes=60 * 2**20
        ),
    )(
        shift_offset, sources.reshape(1, 64), block_ids.reshape(1, 64), norm_gain.reshape(1, 512),
        global_state, regional_state, qkv_weight, out_weight, position_bias.reshape(8, 8, 16, 128),
        jnp.swapaxes(conv_state, 1, 2), cond_weight, conv_mid, conv_out, blocks,
    )
    gnext, rnext = pl.pallas_call(
        hand_over,
        out_shape=[
            jax.ShapeDtypeStruct((16, 64, 512), BF16),
            jax.ShapeDtypeStruct((1584, 128), F32),
        ],
        in_specs=[anywhere, anywhere],
        out_specs=[anywhere, anywhere],
        scratch_shapes=[pltpu.VMEM((16, 64, 512), BF16), pltpu.VMEM((1584, 128), F32), dma((8,)), dma((8,))],
    )(gnext, rnext)
    return gnext, rnext.reshape(99, 16, 128)


def solution(mesh):
    return jax.shard_map(
        on_device,
        mesh=mesh,
        in_specs=(
            P("glob", "reg", None),
            P(), P(), P(), P(),
            P(None, "glob", "reg"),
            P(), P(), P(), P(), P(),
            P("glob", "reg", None),
            P("glob", "reg", None),
            P(),
        ),
        out_specs=(P("glob", "reg", None), P(None, "glob", "reg")),
        check_vma=False,
    )
```

```python
import jax
import jax.numpy as jnp
from jax import lax
from jax.experimental import pallas as pl
from jax.experimental.pallas import tpu as pltpu
from jax.sharding import PartitionSpec as P

MESH = pl.DeviceIdType.MESH
F32 = jnp.float32
BF16 = jnp.bfloat16
NG, NR = 8, 16
PITCH, LEAD = 144, 8
NT = (((1,), (1,)), ((), ()))


def dot(a, b):
    return jnp.dot(a, b, preferred_element_type=F32)


def dot_nt(a, b):
    return lax.dot_general(a, b, NT, preferred_element_type=F32)


def silu(u):
    half = 0.5 * u
    return half + half * jnp.tanh(half)


def rows_at(index, count):
    return pl.ds(pl.multiple_of(index, 16), count)


def body(
    shift_ref, src_ref, bid_ref, gain_ref,
    gs_hbm, rs_hbm, qkvw_hbm, outw_hbm, bias_hbm, cs_hbm, cw_hbm, cm_hbm, co_hbm, blk_hbm,
    gnext_hbm, rnext_hbm,
    own, rsv, qkvw, outw, bias, csv, cw, cmv, cov, blk,
    sb, pb, fb, xb, hb, slab, sg, xn, qk, qkv, qp, kv, biasr, span, packed, onext, yv, sel, zpart, zs, zr, z2, zc, cout, cin,
    st32, edge, el, er, rl, rr, xf, x3, hu, hd, p1, w1, w2, w3, amat, xm, x2, pt, ost,
    lsem, psend, precv, fsend, frecv, esend, erecv, hsend, hrecv, gsend, grecv,
    asend, arecv, bsend, brecv, nsend, nrecv, osem, rounds,
):
    g = lax.axis_index("glob")
    r = lax.axis_index("reg")
    odd = lax.rem(g, 2)
    core = lax.rem(r, 2)
    chip = r // 2
    shift = shift_ref[0]
    partner = (g + 1 - 2 * odd, r)
    ahead = (lax.rem(g + 2 - 4 * odd + NG, NG), r)
    behind = (lax.rem(g - 2 + 4 * odd + NG, NG), r)
    mate = (g, r + 1 - 2 * core)
    up, down = (lax.rem(g + NG - 1, NG), r), (lax.rem(g + 1, NG), r)
    left, right = (g, lax.rem(r + NR - 1, NR)), (g, lax.rem(r + 1, NR))
    chips = [(g, lax.rem(r + 2 * d, NR)) for d in range(1, 8)]
    around = [
        (a, b, (lax.rem(g + a + NG, NG), lax.rem(r + b + NR, NR)))
        for a in (-1, 0, 1) for b in (-1, 0, 1) if (a, b) != (0, 0)
    ]

    bar = pltpu.get_barrier_semaphore()
    greet = [partner, ahead, behind, mate, (g, lax.rem(r + 4, NR)), (g, lax.rem(r + 12, NR)), (g, r + 2 - 4 * lax.rem(chip, 2))]
    for target in greet:
        pl.semaphore_signal(bar, inc=1, device_id=target, device_id_type=MESH)
    def tell(i):
        for target in greet:
            pl.semaphore_signal(rounds.at[i], inc=1, device_id=target, device_id_type=MESH)

    local = [
        (gs_hbm, own), (rs_hbm, rsv), (qkvw_hbm, qkvw), (bias_hbm, bias), (outw_hbm, outw),
        (blk_hbm, blk), (cs_hbm, csv), (cw_hbm, cw), (cm_hbm, cmv), (co_hbm, cov),
    ]
    loads = [pltpu.make_async_copy(a, b, lsem.at[i]) for i, (a, b) in enumerate(local)]
    for copy in loads:
        copy.start()

    def remote(src, dst, ssem, rsem, target):
        return pltpu.make_async_remote_copy(
            src_ref=src, dst_ref=dst, send_sem=ssem, recv_sem=rsem,
            device_id=target, device_id_type=MESH,
        )

    loads[0].wait()
    for i in range(4):
        sb[i] = own[i + jnp.where(i < 8 - shift, 0, 8)]
    slab[...] = jnp.zeros(slab.shape, jnp.int32)
    slab[0:1, 0:64] = src_ref[...]
    sg[chip, core] = slab[...]
    zc[1, 192:256, :] = jnp.zeros((64, 256), BF16)
    for band in (0, 2):
        zc[band, 64:256, :] = jnp.zeros((192, 256), BF16)
    pl.semaphore_wait(bar, len(greet))

    firsts, seconds, forwards, mergeds = [], [], [], []
    for c in range(2):
        at, late = pl.ds(2 * c, 2), pl.ds(4 + 2 * c, 2)
        firsts.append(remote(sb.at[at], pb.at[at], psend.at[c], precv.at[c], partner))
        seconds.append(remote(own.at[pl.ds(4 + 2 * c + 8 * odd, 2)], xb.at[at], psend.at[2 + c], precv.at[2 + c], behind))
        forwards.append(remote(pb.at[at], fb.at[at], fsend.at[c], frecv.at[c], ahead))
        mergeds.append(remote(sb.at[late], hb.at[late], fsend.at[2 + c], frecv.at[2 + c], partner))
    for c in range(2):
        firsts[c].start()
        seconds[c].start()
    mate_slab = remote(slab, sg.at[chip, core], gsend.at[0], grecv.at[0], mate)
    mate_slab.start()
    sends = firsts + seconds + forwards + mergeds + [mate_slab]
    tell(0)

    def pass_on(c):
        firsts[c].wait_recv()
        forwards[c].start()
        seconds[c].wait_recv()
        for i in range(4 + 2 * c, 6 + 2 * c):
            for_partner = own[i + 8 * (1 - odd)]
            from_behind = xb[i - 4]
            up_row = i < 8 - shift
            sb[i] = jnp.where(jnp.where(odd == 1, jnp.logical_not(up_row), up_row), from_behind, for_partner)
        mergeds[c].start()

    loads[1].wait()
    st32[0:1584, :] = rsv[...].reshape(1584, 128).astype(F32)
    st32[1584:2048, :] = jnp.zeros((464, 128), F32)

    def turn(y, _):
        cells = st32[pl.ds(y, 128, stride=16), :].T
        xf[pl.ds(pl.multiple_of(y * PITCH + LEAD, 8), 128), :] = cells
        at = pl.ds(pl.multiple_of(y * 8, 8), 8)
        edge[0, at, :] = cells[0:8]
        edge[1, at, :] = cells[120:128]
        return 0

    lax.fori_loop(0, 16, turn, 0, unroll=True)
    el[...] = edge[0].astype(BF16)
    er[...] = edge[1].astype(BF16)
    edges = [
        remote(el, rr, esend.at[0], erecv.at[0], left),
        remote(er, rl, esend.at[1], erecv.at[1], right),
    ]
    pl.semaphore_wait(rounds.at[0], len(greet))
    tell(1)

    low = lax.broadcasted_iota(jnp.int32, (128, 128), 1) < 64
    upward = [i < 8 - shift for i in range(8)]
    packed_row = [i + jnp.where(upward[i], 0, 8) for i in range(8)]

    def project(tokens, at, first):
        count = tokens.shape[0] * 64
        for w in range(0, count, 128):
            values = tokens[w // 64 : w // 64 + 2].reshape(128, 512).astype(F32)
            center = values - jnp.mean(values, axis=-1, keepdims=True)
            spread = jnp.mean(center * center, axis=-1, keepdims=True)
            xn[w : w + 128, :] = (center * lax.rsqrt(spread + 1e-05) * gain_ref[...]).astype(BF16)
        for n in range(first, 3):
            part = dot(xn[0:count, :], qkvw[:, n * 512 : n * 512 + 512]).astype(BF16)
            if n == 0:
                part = (part * 0.125).astype(BF16)
            qk[at : at + count // 64, :, n * 512 : n * 512 + 512] = part.reshape(count // 64, 64, 512)

    places = [(w, hp) for w in range(4) for hp in range(4)]

    def two_heads(q):
        zero = jnp.zeros_like(q)
        return jnp.concatenate([jnp.where(low, q, zero), jnp.where(low, zero, q)], axis=0)

    def keep(w, hp, mixed):
        for j in range(8):
            span[j, w * 16 : w * 16 + 16, hp * 128 : hp * 128 + 128] = mixed[j * 16 : j * 16 + 16]

    def attend_inner():
        for j in range(8):
            row = qk[8 - shift + j]
            for w in range(4):
                qkv[w * 128 + j * 16 : w * 128 + j * 16 + 16, :] = row[w * 16 : w * 16 + 16, :]
        ones = jnp.ones((128, 128), BF16)
        scores = []
        for w, hp in places:
            q = qkv[w * 128 : w * 128 + 128, hp * 128 : hp * 128 + 128]
            key = qkv[w * 128 : w * 128 + 128, 512 + hp * 128 : 512 + hp * 128 + 128]
            scores.append(dot_nt(two_heads(q), key))
        weights = []
        for (w, hp), score in zip(places, scores):
            score = score + bias[2 * hp : 2 * hp + 2].reshape(256, 128)
            weights.append(jnp.exp(score - jnp.max(score, axis=-1, keepdims=True)).astype(BF16))
        sums = []
        for (w, hp), weight in zip(places, weights):
            val = qkv[w * 128 : w * 128 + 128, 1024 + hp * 128 : 1024 + hp * 128 + 128]
            sums.append(dot(weight, jnp.concatenate([val, ones], axis=1)))
        for (w, hp), both in zip(places, sums):
            top = jnp.where(low, both[0:128, 0:128], both[128:256, 0:128])
            under = jnp.where(low, both[0:128, 128:256], both[128:256, 128:256])
            keep(w, hp, (top / under).astype(BF16))

    def cross_setup():
        for i in range(8):
            row = qk[packed_row[i], :, 0:512]
            for w in range(4):
                qp[w * 128 + i * 16 : w * 128 + i * 16 + 16, :] = row[w * 16 : w * 16 + 16, :]
        first = lax.broadcasted_iota(jnp.int32, (16, 128), 1) // 16 < shift
        for i in range(8):
            above = jnp.where((g == 0) & first, -jnp.inf, 0.0)
            below = jnp.where((g < NG - 1) | first, 0.0, -jnp.inf)
            absent = jnp.where(upward[i], above, below).astype(F32)
            at = i + shift - jnp.where(i + shift >= 8, 8, 0)
            for h in range(8):
                biasr[h, i * 16 : i * 16 + 16, :] = bias[h, at] + absent

    def attend_cross():
        for j in range(8):
            rows = (
                qk[jnp.where(j < shift, 24 - shift + j, j - shift), :, 512:1536],
                qk[jnp.where(j < shift, 16 - shift + j, 16 + j - shift), :, 512:1536],
            )
            for k in range(2):
                for w in range(4):
                    at = w * 256 + k * 128 + j * 16
                    kv[at : at + 16, :] = rows[k][w * 16 : w * 16 + 16, :]
        upper = (lax.broadcasted_iota(jnp.int32, (256, 128), 0) // 16) % 8 < 8 - shift
        scores = []
        for w, hp in places:
            q = qp[w * 128 : w * 128 + 128, hp * 128 : hp * 128 + 128]
            scores.append(dot_nt(two_heads(q), kv[w * 256 : w * 256 + 256, hp * 128 : hp * 128 + 128]))
        weights, sums = [], []
        for (w, hp), score in zip(places, scores):
            score = jnp.where(upper, score[:, 0:128], score[:, 128:256])
            score = score + biasr[2 * hp : 2 * hp + 2].reshape(256, 128)
            weight = jnp.exp(score - jnp.max(score, axis=-1, keepdims=True))
            sums.append(jnp.sum(weight, axis=-1, keepdims=True))
            weights.append(weight.astype(BF16))
        mixes = []
        for (w, hp), weight in zip(places, weights):
            cols = slice(512 + hp * 128, 512 + hp * 128 + 128)
            vals = [kv[w * 256 + k * 128 : w * 256 + k * 128 + 128, cols] for k in range(2)]
            mixes.append(dot(weight, jnp.concatenate(vals, axis=1)))
        for (w, hp), mix, total in zip(places, mixes, sums):
            mix = jnp.where(upper, mix[:, 0:128], mix[:, 128:256]) / total
            keep(w, hp, jnp.where(low, mix[0:128], mix[128:256]).astype(BF16))

    def update(at, index):
        change = dot(span[...].reshape(512, 512), outw[...])
        for i in range(8):
            mine = own[index(i)].astype(F32) + change[i * 64 : i * 64 + 64]
            packed[at + i] = mine.astype(BF16)
        tokens = packed[at : at + 8].reshape(512, 512)
        yv[at * 64 : at * 64 + 512, :] = dot_nt(tokens, cw[...]).astype(BF16)

    loads[2].wait()
    project(own[...], 0, 0)
    pass_on(0)
    pl.semaphore_wait(rounds.at[1], len(greet))
    tell(2)
    for copy in edges:
        copy.start()
    mate_slab.wait_recv()
    slabs = [
        remote(sg.at[chip], sg.at[chip], gsend.at[1 + i], grecv.at[1 + i], t) for i, t in enumerate(chips)
    ]
    for copy in slabs:
        copy.start()
    sends += edges + slabs
    for i in range(3, 10):
        loads[i].wait()
    attend_inner()
    update(8, lambda j: 8 - shift + j)
    cross_setup()
    pl.semaphore_wait(rounds.at[2], len(greet))
    tell(3)

    for o in range(9):
        w1[o * 128 : o * 128 + 128, :] = jnp.concatenate(
            [csv[o].astype(F32), jnp.zeros((29, 256), F32)], axis=0
        ).astype(BF16)
        w2[:, o * 256 : o * 256 + 256] = cmv[o]
        a, b = o // 3, o % 3
        w3[b * 128 : b * 128 + 128, a * 256 : a * 256 + 256] = jnp.concatenate(
            [cov[o].astype(F32), jnp.zeros((29, 256), F32)], axis=0
        ).astype(BF16)

    def interpolation(y, _):
        part = blk[:, pl.ds(pl.multiple_of(y * 128, 128), 128)].astype(F32)
        cells = jnp.concatenate([part, jnp.zeros((64, 128), F32)], axis=0).T
        main = jnp.concatenate(
            [pltpu.roll(cells[120:128], 64, 1), cells, jnp.zeros((8, 128), F32)], axis=0
        )
        side = jnp.concatenate([jnp.zeros((136, 128), F32), cells[0:8]], axis=0)
        amat[rows_at(y * PITCH, PITCH), :] = jnp.concatenate([main, side], axis=1).astype(BF16)
        return 0

    lax.fori_loop(0, 16, interpolation, 0, unroll=True)
    pass_on(1)

    for copy in edges:
        copy.wait_recv()
    edge[0] = jnp.where(r > 0, rl[...].astype(F32), 0.0)
    edge[1] = jnp.where(r < NR - 1, rr[...].astype(F32), 0.0)

    def spread3(cells):
        width = cells.shape[0]
        return jnp.concatenate([pltpu.roll(cells, 1, 0), cells, pltpu.roll(cells, width - 1, 0)], axis=1).astype(BF16)

    def frame(y, _):
        at = pl.ds(pl.multiple_of(y * 8, 8), 8)
        main = xf[pl.ds(pl.multiple_of(y * PITCH + LEAD, 8), 128), :]
        cells = jnp.concatenate([edge[0, at, :], main, edge[1, at, :]], axis=0)
        x3[rows_at((y + 3) * PITCH, PITCH), :] = spread3(cells)
        return 0

    lax.fori_loop(0, 16, frame, 0, unroll=True)
    borders = [
        remote(x3.at[pl.ds(3 * PITCH, 3 * PITCH), pl.ds(128, 128)], hd, hsend.at[0], hrecv.at[0], up),
        remote(x3.at[pl.ds(16 * PITCH, 3 * PITCH), pl.ds(128, 128)], hu, hsend.at[1], hrecv.at[1], down),
    ]

    def first_conv(y0, count):
        parts = [x3[rows_at((y0 + a) * PITCH, count * PITCH), :] for a in range(3)]
        p1[rows_at(y0 * PITCH, count * PITCH), :] = dot(jnp.concatenate(parts, axis=1), w1[...])

    lax.fori_loop(0, 2, lambda i, _: (first_conv(3 + 7 * i, 7), 0)[1], 0, unroll=True)

    for copy in slabs:
        copy.wait_recv()
    ids = sg[...].reshape(128, 128)[0:128]
    ids = jnp.concatenate([ids[8 * j : 8 * j + 1] for j in range(16)], axis=0)
    row = lax.shift_right_logical(ids, 10) - 16 * g
    col = jnp.bitwise_and(ids, 1023) - 64 * r
    row = jnp.where(row < 8 - shift, row, jnp.where(row >= 16 - shift, row - 8, row + shift))
    token = jnp.where((col >= 0) & (col < 64), row * 64 + col, -1).astype(F32)
    token = jnp.concatenate([token, jnp.zeros((112, 128), F32)], axis=0).T
    position = lax.broadcasted_iota(jnp.int32, (64, 1024), 1).astype(F32)
    for j in range(16):
        hit = token[0:64, j : j + 1] == position
        sel[j % 2, (j // 2) * 64 : (j // 2) * 64 + 64, :] = jnp.where(hit, 1.0, 0.0).astype(BF16)
    for half in range(2):
        zpart[half] = dot(sel[half, :, 512:1024], yv[512:1024, :])
    slots = lax.broadcasted_iota(jnp.int32, (64, 64), 0)
    perm = jnp.where(slots == bid_ref[...], 1.0, 0.0).astype(BF16)

    pl.semaphore_wait(rounds.at[3], len(greet))

    for copy in forwards + mergeds:
        copy.wait_recv()
    for copy in borders:
        copy.start()
    sends += borders
    for i in range(4):
        hb[i] = jnp.where(jnp.where(odd == 1, upward[i], jnp.logical_not(upward[i])), fb[i], pb[i])
    project(hb[...], 16, 1)
    attend_cross()

    update(0, lambda i: packed_row[i])

    def contribution(half):
        zs[half] = (zpart[half] + dot(sel[half, :, 0:512], yv[0:512, :])).astype(BF16)

    contribution(1 - core)
    to_mate = remote(zs.at[1 - core], zr, asend, arecv, mate)
    to_mate.start()
    contribution(core)
    for i in range(16):
        onext[i] = packed[jnp.where(i < 8 - shift, i, jnp.where(i >= 16 - shift, i - 8, i + shift))]
    store_g = pltpu.make_async_copy(onext, gnext_hbm, osem.at[0])
    store_g.start()
    to_mate.wait()
    zs[core] = zs[core] + zr[...]
    tiles = []
    for i, t in enumerate(chips):
        q = lax.rem(chip + i + 1, 8)
        tiles.append(remote(zs.at[core, rows_at(q * 64, 64)], z2.at[i], bsend.at[i], brecv.at[i], t))
    for copy in tiles:
        copy.start()
    for copy in borders:
        copy.wait_recv()
    for a in range(3):
        at = pl.ds(a * PITCH, PITCH)
        x3[a * PITCH : (a + 1) * PITCH, :] = spread3(jnp.where(g > 0, hu[at, :].astype(F32), 0.0))
        x3[(19 + a) * PITCH : (20 + a) * PITCH, :] = spread3(jnp.where(g < NG - 1, hd[at, :].astype(F32), 0.0))
    lax.fori_loop(0, 2, lambda i, _: (first_conv(17 * i, 3), 0)[1], 0, unroll=True)
    total = zs[core, rows_at(chip * 64, 64), :].astype(F32)
    for copy in tiles:
        copy.wait()
    for i in range(7):
        total = total + z2[i].astype(F32)
    zc[1, 0:64, :] = dot(perm, total.astype(BF16)).astype(BF16)
    corner_rows = [amat[y * PITCH + at : y * PITCH + at + 16, 0:64] for y in (0, 1, 14, 15) for at in (0, PITCH - 16)]
    corners = dot(jnp.concatenate(corner_rows, axis=0), zc[1, 0:64])
    for i in range(4):
        at = [(4 * (i // 2) + 2 * n + i % 2) * 16 + 8 * (1 - i % 2) for n in range(2)]
        cout[i] = jnp.concatenate([corners[at[0] : at[0] + 8], corners[at[1] : at[1] + 8]], axis=0).astype(BF16)
    ring = []
    for i, (a, b, t) in enumerate(around):
        if a and b:
            here, there = (1 + a) + (1 + b) // 2, (1 - a) + (1 - b) // 2
            ring.append(remote(cout.at[here], cin.at[there], nsend.at[i], nrecv.at[i], t))
        else:
            at = pl.ds((0, 64, 128)[b], 64)
            ring.append(remote(zc.at[1, pl.ds(0, 64)], zc.at[1 - a, at], nsend.at[i], nrecv.at[i], t))
    for copy in ring:
        copy.start()
    sends += ring

    cell = lax.broadcasted_iota(jnp.int32, (PITCH, 256), 0)
    across = ((cell >= LEAD) | (r > 0)) & ((cell < LEAD + 128) | (r < NR - 1))

    def on_grid(values, y):
        here = 16 * g + y
        return jnp.where(across & (here >= 0) & (here < 16 * NG), values, 0.0)

    for y0 in range(0, 16, 4):
        size = 4 * PITCH
        at = pl.ds(y0 * PITCH, size)
        u = p1[(y0 + 2) * PITCH : (y0 + 2) * PITCH + size, :] + dot(amat[at, 0:64], zc[1, 0:64])
        u = silu(u)
        for i in range(4):
            xm[(y0 + 2 + i) * PITCH : (y0 + 3 + i) * PITCH, :] = spread3(u[i * PITCH : (i + 1) * PITCH])

    def second_inner(y0, count):
        parts = [
            jnp.concatenate([xm[(y0 + i + a) * PITCH + 16 : (y0 + i + a) * PITCH + 128, :] for i in range(count)], axis=0)
            for a in range(3)
        ]
        u = silu(dot_nt(jnp.concatenate(parts, axis=1), w2[...])).astype(BF16)
        for i in range(count):
            x2[(y0 + i) * PITCH + 16 : (y0 + i) * PITCH + 128, :] = u[i * 112 : i * 112 + 112]

    second_inner(2, 7)
    second_inner(9, 7)

    def last_terms(cells):
        parts = [jnp.concatenate([x2[(y + a) * PITCH + p : (y + a) * PITCH + p + n, :] for y, p, n in cells], axis=0) for a in range(3)]
        terms = dot_nt(jnp.concatenate(parts, axis=1), w3[...])
        start = 0
        for y, p, n in cells:
            pt[y * PITCH + p : y * PITCH + p + n, :] = terms[start : start + n]
            start += n

    last_terms([(y, 16, 112) for y in range(2, 8)])
    last_terms([(y, 16, 112) for y in range(8, 14)])

    for copy in ring:
        copy.wait_recv()

    def first_rows(y0, a0, band):
        size = 2 * PITCH
        u = p1[(y0 + 2) * PITCH : (y0 + 2) * PITCH + size, :] + dot(amat[a0 * PITCH : a0 * PITCH + size, :], zc[band])
        ends = [cin[band + side].astype(F32) for side in range(2)]
        for i in range(2):
            cond = jnp.concatenate(
                [ends[0][8 * i : 8 * i + 8], jnp.zeros((128, 256), F32), ends[1][8 * i : 8 * i + 8]], axis=0
            )
            cells = on_grid(silu(u[i * PITCH : (i + 1) * PITCH] + cond), y0 + i)
            xm[(y0 + 2 + i) * PITCH : (y0 + 3 + i) * PITCH, :] = spread3(cells)

    first_rows(-2, 14, 0)
    first_rows(16, 0, 2)

    def edge_cells(ref, y, width):
        return [ref[y * PITCH : y * PITCH + width, :], ref[(y + 1) * PITCH - width : (y + 1) * PITCH, :]]

    own_part = jnp.concatenate([c for y in range(2, 18) for c in edge_cells(p1, y, 32)], axis=0)
    tile_part = jnp.concatenate([c for y in range(16) for c in edge_cells(amat, y, 32)], axis=0)
    u = silu(own_part + dot(tile_part, zc[1]))
    for y in range(16):
        for side in range(2):
            cells = u[(2 * y + side) * 32 : (2 * y + side) * 32 + 32]
            inside = across[0:32] if side == 0 else across[PITCH - 32 : PITCH]
            cells = spread3(jnp.where(inside, cells, 0.0))
            at = (y + 2) * PITCH + (0 if side == 0 else PITCH - 16)
            xm[at : at + 16, :] = cells[0:16] if side == 0 else cells[16:32]

    def second_rows(y0):
        parts = [xm[(y0 + a) * PITCH : (y0 + a + 2) * PITCH, :] for a in range(3)]
        u = silu(dot_nt(jnp.concatenate(parts, axis=1), w2[...]))
        for i in range(2):
            cells = on_grid(u[i * PITCH : (i + 1) * PITCH], y0 + i - 1)
            x2[(y0 + i) * PITCH : (y0 + i + 1) * PITCH, :] = cells.astype(BF16)

    second_rows(0)
    second_rows(16)
    parts = [jnp.concatenate([c for y in range(2, 16) for c in edge_cells(xm, y + a, 16)], axis=0) for a in range(3)]
    u = silu(dot_nt(jnp.concatenate(parts, axis=1), w2[...]))
    for y in range(2, 16):
        for side in range(2):
            cells = u[(y - 2) * 32 + side * 16 : (y - 2) * 32 + side * 16 + 16]
            inside = across[0:16] if side == 0 else across[PITCH - 16 : PITCH]
            at = y * PITCH + (0 if side == 0 else PITCH - 16)
            x2[at : at + 16, :] = jnp.where(inside, cells, 0.0).astype(BF16)

    last_terms([(y, 0, PITCH) for y in (0, 1, 14, 15)] + [(y, p, 16) for y in range(2, 14) for p in (0, PITCH - 16)])
    for y in range(16):
        t = pt[y * PITCH : (y + 1) * PITCH, :]
        total = pltpu.roll(t[:, 0:128], 1, 0) + t[:, 128:256] + pltpu.roll(t[:, 256:384], PITCH - 1, 0)
        at = pl.ds(y, 128, stride=16)
        ost[at, :] = st32[at, :] + total[LEAD : LEAD + 128].T
    store_r = pltpu.make_async_copy(ost.at[pl.ds(0, 1584)], rnext_hbm, osem.at[1])
    store_r.start()
    for copy in sends:
        copy.wait_send()
    store_g.wait()
    store_r.wait()


def hand_over(gnext_in, rnext_in, gnext_out, rnext_out, gbuf, rbuf, isem, osem):
    pairs = []
    for i in range(4):
        at, rows = pl.ds(4 * i, 4), pl.ds(400 * i, 400 if i < 3 else 384)
        for n, (a, b, c, part) in enumerate(((gnext_in, gbuf, gnext_out, at), (rnext_in, rbuf, rnext_out, rows))):
            first = pltpu.make_async_copy(a.at[part], b.at[part], isem.at[2 * i + n])
            pairs.append((first, pltpu.make_async_copy(b.at[part], c.at[part], osem.at[2 * i + n])))
    for first, _ in pairs:
        first.start()
    for first, second in pairs:
        first.wait()
        second.start()
    for _, second in pairs:
        second.wait()


def on_device(
    global_state, norm_gain, qkv_weight, out_weight, position_bias, regional_state,
    conv_state, cond_weight, conv_mid, conv_out, blocks, sources, block_ids, shift_offset,
):
    vm, anywhere = pl.BlockSpec(memory_space=pltpu.VMEM), pl.BlockSpec(memory_space=pl.ANY)
    dma = pltpu.SemaphoreType.DMA
    scratch = [
        ((16, 64, 512), BF16), ((99, 16, 128), BF16), ((512, 1536), BF16), ((512, 512), BF16),
        ((8, 8, 16, 128), F32), ((9, 99, 256), BF16), ((256, 512), BF16), ((9, 256, 256), BF16),
        ((9, 99, 256), BF16), ((64, 2048), BF16),
        ((8, 64, 512), BF16), ((4, 64, 512), BF16), ((4, 64, 512), BF16),
        ((4, 64, 512), BF16), ((8, 64, 512), BF16),
        ((8, 128), jnp.int32), ((8, 2, 8, 128), jnp.int32),
        ((1024, 512), BF16), ((24, 64, 1536), BF16), ((512, 1536), BF16),
        ((512, 512), BF16), ((1024, 1024), BF16), ((8, 128, 128), F32),
        ((8, 64, 512), BF16), ((16, 64, 512), BF16), ((16, 64, 512), BF16), ((1024, 256), BF16),
        ((2, 512, 1024), BF16), ((2, 512, 256), F32), ((2, 512, 256), BF16), ((512, 256), BF16),
        ((7, 64, 256), BF16), ((3, 256, 256), BF16), ((4, 16, 256), BF16), ((4, 16, 256), BF16),
        ((2048, 128), F32), ((2, 128, 128), F32),
        ((128, 128), BF16), ((128, 128), BF16), ((128, 128), BF16), ((128, 128), BF16),
        ((16 * PITCH, 128), F32), ((22 * PITCH, 384), BF16),
        ((3 * PITCH, 128), BF16), ((3 * PITCH, 128), BF16), ((20 * PITCH, 256), F32),
        ((1152, 256), BF16), ((256, 2304), BF16), ((384, 768), BF16),
        ((16 * PITCH, 256), BF16), ((20 * PITCH, 768), BF16), ((18 * PITCH, 256), BF16),
        ((16 * PITCH, 384), F32), ((2048, 128), F32),
    ]
    counts = [10, 4, 4, 4, 4, 2, 2, 2, 2, 8, 8, 0, 0, 7, 7, 8, 8, 2]
    gnext, rnext = pl.pallas_call(
        body,
        out_shape=[
            jax.ShapeDtypeStruct((16, 64, 512), BF16),
            jax.ShapeDtypeStruct((1584, 128), F32),
        ],
        in_specs=[pl.BlockSpec(memory_space=pltpu.SMEM)] + [vm] * 3 + [anywhere] * 10,
        out_specs=[anywhere, anywhere],
        scratch_shapes=[pltpu.VMEM(*s) for s in scratch] + [dma((n,)) if n else dma for n in counts] + [pltpu.SemaphoreType.REGULAR((4,))],
        compiler_params=pltpu.CompilerParams(
            collective_id=0, has_side_effects=True, vmem_limit_bytes=60 * 2**20
        ),
    )(
        shift_offset, sources.reshape(1, 64), block_ids.reshape(1, 64), norm_gain.reshape(1, 512),
        global_state, regional_state, qkv_weight, out_weight, position_bias.reshape(8, 8, 16, 128),
        jnp.swapaxes(conv_state, 1, 2), cond_weight, conv_mid, conv_out, blocks,
    )
    gnext, rnext = pl.pallas_call(
        hand_over,
        out_shape=[
            jax.ShapeDtypeStruct((16, 64, 512), BF16),
            jax.ShapeDtypeStruct((1584, 128), F32),
        ],
        in_specs=[anywhere, anywhere],
        out_specs=[anywhere, anywhere],
        scratch_shapes=[pltpu.VMEM((16, 64, 512), BF16), pltpu.VMEM((1584, 128), F32), dma((8,)), dma((8,))],
    )(gnext, rnext)
    return gnext, rnext.reshape(99, 16, 128)


def solution(mesh):
    return jax.shard_map(
        on_device,
        mesh=mesh,
        in_specs=(
            P("glob", "reg", None),
            P(), P(), P(), P(),
            P(None, "glob", "reg"),
            P(), P(), P(), P(), P(),
            P("glob", "reg", None),
            P("glob", "reg", None),
            P(),
        ),
        out_specs=(P("glob", "reg", None), P(None, "glob", "reg")),
        check_vma=False,
    )
```
